512 devices in a mesh: dp: 32 (over y, x), tensor: 16 (over z, core).
Axes of the slice: x: 4, y: 8, z: 8, core: 2. Of those that a mesh axis runs over, the one named last changes fastest.
Arguments:
- gradient: bfloat16 [32, 4096, 4096], P('dp', 'tensor'), may hold values from -20 to 20, as said below
- error_buffer: bfloat16 [32, 4096, 4096], P('dp', 'tensor'), may hold values from -1.5 to 1.5
- right_start: float32 [8, 4096], replicated, may hold values from -6 to 6
Outputs:
- update: float32 [4096, 4096], P('tensor', 'dp')
- left_factor: float32 [8, 4096], P(None, 'tensor')
- right_factor: float32 [8, 4096], replicated
The draws below stay inside these ranges and needn't reach their ends.
Inputs may be any that keep to these rules, and one draw needn't show every extreme that they name: Entries of the gradient are real-valued with no zeros in bulk.
All inputs are finite; a program needn't handle non-finite values.
Results may differ from the reference program's by a relative error of at most 0.0003.
Values sent between devices are 32-bit elements; how exact they have to be, the bound alone decides.
No kernel may reach another device: no remote copies, remote signals or barrier semaphores. Data moves between devices by JAX's collectives and lax.ppermute only.
A program may use at most 64 MiB of HBM per device.

```python
import jax
import jax.numpy as jnp
from jax import lax

D_IN = 4096
D_OUT = 4096
RANK = 8
REPLICAS = 32


def draw_gradient(key, part):
    key = jax.random.fold_in(key, 1)
    keys = jax.random.split(key, 4)
    steps = jnp.arange(REPLICAS).astype(jnp.float32) / max(REPLICAS - 1, 1)
    replica_scale = jnp.exp(jnp.log(3.0) * steps) * jax.random.uniform(keys[0], (REPLICAS,), jnp.float32, 0.8, 1.2)
    row_scale = jnp.exp(jax.random.uniform(keys[1], (1, D_OUT, 1), jnp.float32, 0.0, jnp.log(10.0)))
    col_scale = jnp.exp(jax.random.uniform(keys[2], (1, 1, D_IN), jnp.float32, jnp.log(0.5), jnp.log(2.0)))
    base = jnp.clip(jax.random.normal(keys[3], (REPLICAS, D_OUT, D_IN), jnp.float32), -5.0, 5.0)
    values = 0.05 * base * replica_scale[:, None, None] * row_scale * col_scale
    return values.astype(jnp.bfloat16)


def levels(key, shape, cuts, least, largest):
    level, own = 1.0, jax.random.fold_in(key, 6)
    for dim, blocks in cuts:
        draws = jnp.exp(jax.random.uniform(jax.random.fold_in(own, dim), (blocks,), jnp.float32, least / len(cuts), largest / len(cuts)))
        level = level * jnp.repeat(draws, shape[dim] // blocks).reshape([-1 if axis == dim else 1 for axis in range(len(shape))])
    return level


def centred(rng, dims, spread, limit, pieces=(), dtype=jnp.bfloat16):
    values = jax.random.normal(rng, dims, jnp.float32) * spread
    if len(pieces) > 0:
        values = levels(rng, dims, pieces, -0.22, 0.18) * values
    return jnp.clip(values, min=-limit, max=limit).astype(dtype)


def setup_inputs(seed: int = 0) -> dict:
    seeds = jax.random.split(jax.random.key(seed), 4)
    return {
        "gradient": draw_gradient(jax.random.fold_in(seeds[3], 71), 0),
        "error_buffer": centred(seeds[1], (REPLICAS, D_OUT, D_IN), 0.1, 1.5, ((0, 32), (1, 16))),
        "right_start": centred(seeds[2], (RANK, D_IN), 1.0, 6.0, (), jnp.float32),
    }


def lower_solve(chol, values):
    solved = []
    for index in range(chol.shape[0]):
        accum = values[index]
        for inner in range(index):
            accum = accum - chol[index, inner] * solved[inner]
        solved.append(accum / chol[index, index])
    return jnp.stack(solved)

def reference(gradient, error_buffer, right_start):
    count = gradient.shape[0]
    high = lax.Precision.HIGHEST

    def left_term(pair):
        corrected = pair[0].astype(jnp.float32) + pair[1].astype(jnp.float32)
        return jnp.dot(right_start, corrected.T, precision=high)
    left_sum = jnp.sum(lax.map(left_term, (gradient, error_buffer)), axis=0)
    gram = jnp.dot(left_sum, left_sum.T, precision=high)
    chol = jnp.linalg.cholesky(gram)
    left_factor = lower_solve(chol, left_sum)

    def right_term(pair):
        corrected = pair[0].astype(jnp.float32) + pair[1].astype(jnp.float32)
        return jnp.dot(left_factor, corrected, precision=high)
    right_factor = jnp.sum(lax.map(right_term, (gradient, error_buffer)), axis=0) / count
    update = jnp.dot(left_factor.T, right_factor, precision=high)
    return (update, left_factor, right_factor)
```

```python
import jax
import jax.numpy as jnp
from jax import lax
from jax.sharding import PartitionSpec as P

HIGH = lax.Precision.HIGHEST


def share(block, axis):
    count = lax.axis_size(axis)
    copies = jnp.broadcast_to(block[None], (count,) + block.shape)
    return lax.all_to_all(copies, axis, 0, 0)


def eliminate(gram, values):
    rank = gram.shape[0]
    rows = jnp.concatenate([gram, values], axis=1)
    index = jnp.arange(rank)[:, None]
    for step in range(rank):
        pivot_row = rows[step : step + 1] / jnp.sqrt(rows[step, step])
        factor = jnp.where(index > step, rows[:, step : step + 1] / jnp.sqrt(rows[step, step]), 0.0)
        rows = jnp.where(index == step, pivot_row, rows - factor * pivot_row)
    return rows[:, rank:]


def on_device(gradient, error_buffer, right_start):
    replicas, shards = lax.axis_size("dp"), lax.axis_size("tensor")
    rank, columns = right_start.shape
    corrected = gradient[0].astype(jnp.float32) + error_buffer[0].astype(jnp.float32)
    left_local = jnp.dot(right_start, corrected.T, precision=HIGH)
    left_sum = jnp.sum(share(left_local, "dp"), axis=0)
    gram_local = jnp.dot(left_sum, left_sum.T, precision=HIGH)
    raw_local = jnp.dot(left_sum, corrected, precision=HIGH)

    width = columns // shards
    blocks = jnp.swapaxes(raw_local.reshape(rank, shards, width), 0, 1)
    grams = jnp.broadcast_to(gram_local[None], (shards, rank, rank))
    grams = jnp.pad(grams, ((0, 0), (0, 0), (0, 128 - rank)))
    sent = jnp.concatenate([blocks, grams], axis=2)
    got = jnp.sum(lax.all_to_all(sent, "tensor", 0, 0), axis=0)
    raw_block, gram = got[:, :width], got[:, width : width + rank]
    raw_block = jnp.sum(share(raw_block, "dp"), axis=0)

    solved = eliminate(gram, jnp.concatenate([left_sum, raw_block / replicas], axis=1))
    left_factor, right_block = solved[:, : left_sum.shape[1]], solved[:, left_sum.shape[1] :]
    right_factor = jnp.swapaxes(share(right_block, "tensor"), 0, 1).reshape(rank, columns)
    column_count = columns // replicas
    right_own = lax.dynamic_slice_in_dim(right_factor, lax.axis_index("dp") * column_count, column_count, 1)
    update = jnp.dot(left_factor.T, right_own, precision=HIGH)
    return (update, left_factor, right_factor)


def solution(mesh):
    return jax.shard_map(
        on_device,
        mesh=mesh,
        in_specs=(P("dp", "tensor", None), P("dp", "tensor", None), P()),
        out_specs=(P("tensor", "dp"), P(None, "tensor"), P()),
        check_vma=False,
    )
```

```python
import functools

import jax
import jax.numpy as jnp
from jax import lax
from jax.experimental import pallas as pl
from jax.experimental.pallas import tpu as pltpu
from jax.sharding import PartitionSpec as P

HIGH = lax.Precision.HIGHEST
F32 = jnp.float32
BF16 = jnp.bfloat16
LANES = 128
VMEM = pl.BlockSpec(memory_space=pltpu.VMEM)
ANY = pl.BlockSpec(memory_space=pl.ANY)


def pieces(values):
    high = values.astype(BF16).astype(F32)
    rest = values - high
    middle = rest.astype(BF16).astype(F32)
    low = rest - middle
    none = jnp.zeros_like(values)
    return jnp.concatenate([high, middle, low, none], axis=0).astype(BF16)


def fold(products, rank):
    return products[:rank] + (products[rank : 2 * rank] + products[2 * rank : 3 * rank])


def left_kernel(chunks, gradient, error, start, out, gradient_here, error_here, arrived):
    copies = []
    rows = gradient.shape[0] // chunks
    for chunk in range(chunks):
        span = pl.ds(chunk * rows, rows)
        pair = []
        for which, (source, target) in enumerate(((gradient, gradient_here), (error, error_here))):
            copy = pltpu.make_async_copy(source.at[span], target.at[span], arrived.at[which, chunk])
            copy.start()
            pair.append(copy)
        copies.append(pair)
    rank = start.shape[0]
    cut = pieces(start[...])
    dims = (((1,), (1,)), ((), ()))
    for chunk in range(chunks):
        for copy in copies[chunk]:
            copy.wait()
        span = slice(chunk * rows, (chunk + 1) * rows)
        total = lax.dot_general(cut, gradient_here[span, :], dims, preferred_element_type=F32)
        total += lax.dot_general(cut, error_here[span, :], dims, preferred_element_type=F32)
        left = fold(total, rank)
        for copy in range(out.shape[0]):
            out[copy, :, span] = left


def left_terms(gradient, error, start, replicas):
    rows, columns = gradient.shape
    rank = start.shape[0]
    chunks = rows // LANES
    return pl.pallas_call(
        functools.partial(left_kernel, chunks),
        out_shape=jax.ShapeDtypeStruct((replicas, rank, rows), F32),
        in_specs=[ANY, ANY, VMEM],
        out_specs=VMEM,
        scratch_shapes=[
            pltpu.VMEM((rows, columns), BF16),
            pltpu.VMEM((rows, columns), BF16),
            pltpu.SemaphoreType.DMA((2, chunks)),
        ],
        compiler_params=pltpu.CompilerParams(vmem_limit_bytes=24 * 2**20),
        name="left_terms",
    )(gradient, error, start)


def raw_kernel(parts, gradient, error, sent, left_out):
    left = jnp.sum(parts[...], axis=0)
    left_out[...] = left
    rank, rows = left.shape
    shards = sent.shape[0]
    width = gradient.shape[1] // shards
    filled = jnp.concatenate([left, jnp.zeros((LANES - rank, rows), F32)], axis=0)
    gram = lax.dot_general(left, filled, (((1,), (1,)), ((), ())), precision=HIGH, preferred_element_type=F32)
    cut = pieces(left)
    for shard in range(shards):
        span = slice(shard * width, (shard + 1) * width)
        total = jnp.dot(cut, gradient[:, span], preferred_element_type=F32)
        total += jnp.dot(cut, error[:, span], preferred_element_type=F32)
        sent[shard, :, :width] = fold(total, rank)
        sent[shard, :, width:] = gram


def raw_terms(parts, gradient, error, shards):
    _, rank, rows = parts.shape
    width = gradient.shape[1] // shards
    return pl.pallas_call(
        raw_kernel,
        out_shape=(
            jax.ShapeDtypeStruct((shards, rank, width + LANES), F32),
            jax.ShapeDtypeStruct((rank, rows), F32),
        ),
        in_specs=[VMEM, VMEM, VMEM],
        out_specs=(VMEM, VMEM),
        compiler_params=pltpu.CompilerParams(vmem_limit_bytes=24 * 2**20),
        name="raw_terms",
    )(parts, gradient, error)


def block_kernel(parts, out, gram):
    total = jnp.sum(parts[...], axis=0)
    width = out.shape[2]
    for copy in range(out.shape[0]):
        out[copy] = total[:, :width]
    gram[...] = total[:, width:]


def block_sum(parts, replicas):
    _, rank, wide = parts.shape
    return pl.pallas_call(
        block_kernel,
        out_shape=(
            jax.ShapeDtypeStruct((replicas, rank, wide - LANES), F32),
            jax.ShapeDtypeStruct((rank, LANES), F32),
        ),
        in_specs=[VMEM],
        out_specs=(VMEM, VMEM),
        name="block_sum",
    )(parts)


def solve_kernel(parts, gram, left, out, left_out):
    replicas = parts.shape[0]
    block = jnp.sum(parts[...], axis=0) * (1.0 / replicas)
    rank, rows = left.shape
    table = jnp.concatenate([gram[...], left[...], block], axis=1)
    index = lax.broadcasted_iota(jnp.int32, table.shape, 0)
    for step in range(rank):
        scale = lax.rsqrt(table[step : step + 1, step : step + 1])
        pivot = table[step : step + 1, :] * scale
        factor = table[:, step : step + 1] * scale
        table = jnp.where(index > step, table - factor * pivot, jnp.where(index == step, pivot, table))
    left_out[...] = table[:, LANES : LANES + rows]
    for copy in range(out.shape[0]):
        out[copy] = table[:, LANES + rows :]


def solve(parts, gram, left, shards):
    _, rank, width = parts.shape
    return pl.pallas_call(
        solve_kernel,
        out_shape=(
            jax.ShapeDtypeStruct((shards, rank, width), F32),
            jax.ShapeDtypeStruct(left.shape, F32),
        ),
        in_specs=[VMEM, VMEM, VMEM],
        out_specs=(VMEM, VMEM),
        name="solve",
    )(parts, gram, left)


def update_kernel(parts, left, update, right):
    shards, _, width = parts.shape
    own = update.shape[1]
    each = width // own
    here = lax.axis_index("dp")
    offset = pl.multiple_of(lax.rem(here, each) * own, own)
    block = parts[here // each, :, pl.ds(offset, own)]
    update[...] = lax.dot_general(left[...], block, (((0,), (0,)), ((), ())), precision=HIGH, preferred_element_type=F32)
    for shard in range(shards):
        right[:, shard * width : (shard + 1) * width] = parts[shard]


def finish(parts, left, own):
    shards, rank, width = parts.shape
    return pl.pallas_call(
        update_kernel,
        out_shape=(
            jax.ShapeDtypeStruct((left.shape[1], own), F32),
            jax.ShapeDtypeStruct((rank, shards * width), F32),
        ),
        in_specs=[VMEM, VMEM],
        out_specs=(VMEM, VMEM),
        name="update",
    )(parts, left)


def on_device(gradient, error_buffer, right_start):
    replicas, shards = lax.axis_size("dp"), lax.axis_size("tensor")
    gradient, error = gradient[0], error_buffer[0]
    lefts = lax.all_to_all(left_terms(gradient, error, right_start, replicas), "dp", 0, 0)
    raws, left_sum = raw_terms(lefts, gradient, error, shards)
    blocks, gram = block_sum(lax.all_to_all(raws, "tensor", 0, 0), replicas)
    rights, left_factor = solve(lax.all_to_all(blocks, "dp", 0, 0), gram, left_sum, shards)
    update, right_factor = finish(lax.all_to_all(rights, "tensor", 0, 0), left_factor, right_start.shape[1] // replicas)
    return (update, left_factor, right_factor)


def solution(mesh):
    return jax.shard_map(
        on_device,
        mesh=mesh,
        in_specs=(P("dp", "tensor", None), P("dp", "tensor", None), P()),
        out_specs=(P("tensor", "dp"), P(None, "tensor"), P()),
        check_vma=False,
    )
```

```python
import functools
import math

import jax
import jax.numpy as jnp
from jax import lax
from jax.experimental import pallas as pl
from jax.experimental.pallas import tpu as pltpu
from jax.sharding import Mesh
from jax.sharding import PartitionSpec as P

HIGH = lax.Precision.HIGHEST
F32 = jnp.float32
BF16 = jnp.bfloat16
LANES = 128
DP = ("yh", "yl", "x")
TENSOR = ("zh", "zl", "core")
NEAR = ("yl", "zl", "x", "core")
FAR = ("yh", "zh")
VMEM = pl.BlockSpec(memory_space=pltpu.VMEM)
SMALL = pltpu.CompilerParams(vmem_limit_bytes=16 * 2**20)


def pieces(values):
    high = values.astype(BF16).astype(F32)
    rest = values - high
    middle = rest.astype(BF16).astype(F32)
    low = rest - middle
    none = jnp.zeros_like(values)
    return jnp.concatenate([high, middle, low, none], axis=0).astype(BF16)


def fold(products, rank):
    return products[:rank] + (products[rank : 2 * rank] + products[2 * rank : 3 * rank])


def left_kernel(gradient, error, start, out, gradient_here, error_here, start_here, arrived):
    copies = []
    for index, (source, target) in enumerate(((start, start_here), (gradient, gradient_here), (error, error_here))):
        copies.append(pltpu.make_async_copy(source, target, arrived.at[index]))
        copies[-1].start()
    rank = start.shape[0]
    copies[0].wait()
    cut = pieces(start_here[...])
    dims = (((1,), (1,)), ((), ()))
    copies[1].wait()
    total = lax.dot_general(cut, gradient_here[...], dims, preferred_element_type=F32)
    copies[2].wait()
    total += lax.dot_general(cut, error_here[...], dims, preferred_element_type=F32)
    left = fold(total, rank)
    for copy in range(out.shape[0]):
        out[copy] = left


def left_terms(gradient, error, start, replicas):
    rows, columns = gradient.shape
    rank = start.shape[0]
    return pl.pallas_call(
        left_kernel,
        out_shape=(
            pltpu.VMEM((replicas, rank, rows), F32),
            pltpu.VMEM((rows, columns), BF16),
            pltpu.VMEM((rows, columns), BF16),
        ),
        in_specs=[pl.BlockSpec(memory_space=pltpu.HBM)] * 3,
        out_specs=(VMEM, VMEM, VMEM),
        scratch_shapes=[pltpu.VMEM((rank, columns), F32), pltpu.SemaphoreType.DMA((3,))],
        compiler_params=SMALL,
        name="left_terms",
    )(*(pltpu.with_memory_space_constraint(array, pltpu.HBM) for array in (gradient, error, start)))


def raw_kernel(parts, gradient, error, sent, left_out):
    left = jnp.sum(parts[...], axis=0)
    left_out[...] = left
    rank, rows = left.shape
    filled = jnp.concatenate([left, jnp.zeros((LANES - rank, rows), F32)], axis=0)
    gram = lax.dot_general(left, filled, (((1,), (1,)), ((), ())), precision=HIGH, preferred_element_type=F32)
    cut = pieces(left)
    width = gradient.shape[1] // sent.shape[0]
    step = 2 * width
    for pair in range(sent.shape[0] // 2):
        span = slice(pair * step, (pair + 1) * step)
        total = jnp.dot(cut, gradient[:, span], preferred_element_type=F32)
        total += jnp.dot(cut, error[:, span], preferred_element_type=F32)
        total = fold(total, rank)
        for half in range(2):
            sent[2 * pair + half, :, :width] = total[:, half * width : (half + 1) * width]
            sent[2 * pair + half, :, width:] = gram


def raw_terms(parts, gradient, error, blocks):
    _, rank, rows = parts.shape
    width = gradient.shape[1] // blocks
    return pl.pallas_call(
        raw_kernel,
        out_shape=(
            pltpu.VMEM((blocks, rank, width + LANES), F32),
            pltpu.VMEM((rank, rows), F32),
        ),
        in_specs=[VMEM, VMEM, VMEM],
        out_specs=(VMEM, VMEM),
        compiler_params=SMALL,
        name="raw_terms",
    )(parts, gradient, error)


def sum_kernel(parts, out):
    total = jnp.sum(parts[...], axis=0)
    for copy in range(out.shape[0]):
        out[copy] = total


def sum_copies(parts, copies):
    return pl.pallas_call(
        sum_kernel,
        out_shape=pltpu.VMEM((copies,) + parts.shape[1:], F32),
        in_specs=[VMEM],
        out_specs=VMEM,
        compiler_params=SMALL,
        name="sum_copies",
    )(parts)


def solve_kernel(replicas, parts, left, out, left_out):
    total = jnp.sum(parts[...], axis=0) * (1.0 / replicas)
    rank, rows = left.shape
    width = out.shape[2]
    table = jnp.concatenate([total[:, width:], left[...], total[:, :width]], axis=1)
    index = lax.broadcasted_iota(jnp.int32, table.shape, 0)
    for step in range(rank):
        scale = lax.rsqrt(table[step : step + 1, step : step + 1])
        pivot = table[step : step + 1, :] * scale
        factor = table[:, step : step + 1] * scale
        table = jnp.where(index > step, table - factor * pivot, jnp.where(index == step, pivot, table))
    left_out[...] = table[:, LANES : LANES + rows]
    for copy in range(out.shape[0]):
        out[copy] = table[:, LANES + rows :]


def solve(parts, left, blocks, replicas):
    _, rank, wide = parts.shape
    return pl.pallas_call(
        functools.partial(solve_kernel, replicas),
        out_shape=(
            pltpu.VMEM((blocks, rank, wide - LANES), F32),
            pltpu.VMEM(left.shape, F32),
        ),
        in_specs=[VMEM, VMEM],
        out_specs=(VMEM, VMEM),
        compiler_params=SMALL,
        name="solve",
    )(parts, left)


def update_kernel(parts, left, update, left_out, right):
    blocks, _, width = parts.shape
    here = 0
    for axis in DP:
        here = here * lax.axis_size(axis) + lax.axis_index(axis)
    update[...] = lax.dot_general(
        left[...], parts[here], (((0,), (0,)), ((), ())), precision=HIGH, preferred_element_type=F32
    )
    left_out[...] = left[...]
    for block in range(blocks):
        right[:, block * width : (block + 1) * width] = parts[block]


def finish(parts, left):
    blocks, rank, width = parts.shape
    return pl.pallas_call(
        update_kernel,
        out_shape=(
            jax.ShapeDtypeStruct((left.shape[1], width), F32),
            jax.ShapeDtypeStruct(left.shape, F32),
            jax.ShapeDtypeStruct((rank, blocks * width), F32),
        ),
        in_specs=[VMEM, VMEM],
        out_specs=(VMEM, VMEM, VMEM),
        compiler_params=SMALL,
        name="update",
    )(parts, left)


def exchange(blocks, axes):
    return lax.all_to_all(blocks, axes, 0, 0)


def on_device(gradient, error_buffer, right_start):
    replicas, blocks, far = (math.prod(lax.axis_size(axis) for axis in axes) for axes in (DP, NEAR, FAR))
    lefts, gradient, error = left_terms(gradient[0], error_buffer[0], right_start, replicas)
    raws, left_sum = raw_terms(exchange(lefts, DP), gradient, error, blocks)
    sums = sum_copies(exchange(raws, NEAR), far)
    rights, left_factor = solve(exchange(sums, FAR), left_sum, blocks, replicas)
    return finish(exchange(rights, NEAR), left_factor)


def solution(mesh):
    split = Mesh(mesh.devices.reshape(4, 2, 4, 4, 2, 2), ("yh", "yl", "x", "zh", "zl", "core"))
    return jax.shard_map(
        on_device,
        mesh=split,
        in_specs=(P(DP, TENSOR, None), P(DP, TENSOR, None), P()),
        out_specs=(P(TENSOR, DP), P(None, TENSOR), P()),
        check_vma=False,
    )
```

```python
import functools
import math

import jax
import jax.numpy as jnp
from jax import lax
from jax.experimental import pallas as pl
from jax.experimental.pallas import tpu as pltpu
from jax.sharding import Mesh
from jax.sharding import PartitionSpec as P

HIGH = lax.Precision.HIGHEST
F32 = jnp.float32
BF16 = jnp.bfloat16
LANES = 128
DP = ("yh", "yl", "x")
TENSOR = ("zh", "zl", "core")
NEAR = ("yl", "zl", "x", "core")
FAR = ("yh", "zh")
FIRST = {DP: 18, NEAR: 29, FAR: 11}
VMEM = pl.BlockSpec(memory_space=pltpu.VMEM)
SMALL = pltpu.CompilerParams(vmem_limit_bytes=16 * 2**20)


def pieces(values):
    high = values.astype(BF16).astype(F32)
    rest = values - high
    middle = rest.astype(BF16).astype(F32)
    low = rest - middle
    none = jnp.zeros_like(values)
    return jnp.concatenate([high, middle, low, none], axis=0).astype(BF16)


def fold(products, rank):
    return products[:rank] + (products[rank : 2 * rank] + products[2 * rank : 3 * rank])


def left_kernel(gradient, error, start, out, gradient_here, error_here, start_here, arrived):
    copies = []
    for index, (source, target) in enumerate(((start, start_here), (gradient, gradient_here), (error, error_here))):
        copies.append(pltpu.make_async_copy(source, target, arrived.at[index]))
        copies[-1].start()
    rank = start.shape[0]
    copies[0].wait()
    cut = pieces(start_here[...])
    dims = (((1,), (1,)), ((), ()))
    copies[1].wait()
    total = lax.dot_general(cut, gradient_here[...], dims, preferred_element_type=F32)
    copies[2].wait()
    total += lax.dot_general(cut, error_here[...], dims, preferred_element_type=F32)
    left = fold(total, rank)
    for copy in range(out.shape[0]):
        out[copy] = left


def left_terms(gradient, error, start, replicas):
    rows, columns = gradient.shape
    rank = start.shape[0]
    return pl.pallas_call(
        left_kernel,
        out_shape=(
            pltpu.VMEM((replicas, rank, rows), F32),
            pltpu.VMEM((rows, columns), BF16),
            pltpu.VMEM((rows, columns), BF16),
        ),
        in_specs=[pl.BlockSpec(memory_space=pltpu.HBM)] * 3,
        out_specs=(VMEM, VMEM, VMEM),
        scratch_shapes=[pltpu.VMEM((rank, columns), F32), pltpu.SemaphoreType.DMA((3,))],
        compiler_params=SMALL,
        name="left_terms",
    )(*(pltpu.with_memory_space_constraint(array, pltpu.HBM) for array in (gradient, error, start)))


def raw_kernel(parts, gradient, error, sent, left_out):
    left = jnp.sum(parts[...], axis=0)
    left_out[...] = left
    rank, rows = left.shape
    filled = jnp.concatenate([left, jnp.zeros((LANES - rank, rows), F32)], axis=0)
    gram = lax.dot_general(left, filled, (((1,), (1,)), ((), ())), precision=HIGH, preferred_element_type=F32)
    cut = pieces(left)
    width = gradient.shape[1] // sent.shape[0]
    step = 2 * width
    for pair in range(sent.shape[0] // 2):
        span = slice(pair * step, (pair + 1) * step)
        total = jnp.dot(cut, gradient[:, span], preferred_element_type=F32)
        total += jnp.dot(cut, error[:, span], preferred_element_type=F32)
        total = fold(total, rank)
        for half in range(2):
            sent[2 * pair + half, :, :width] = total[:, half * width : (half + 1) * width]
            sent[2 * pair + half, :, width:] = gram


def raw_terms(parts, gradient, error, blocks):
    _, rank, rows = parts.shape
    width = gradient.shape[1] // blocks
    return pl.pallas_call(
        raw_kernel,
        out_shape=(
            pltpu.VMEM((blocks, rank, width + LANES), F32),
            pltpu.VMEM((rank, rows), F32),
        ),
        in_specs=[VMEM, VMEM, VMEM],
        out_specs=(VMEM, VMEM),
        compiler_params=SMALL,
        name="raw_terms",
    )(parts, gradient, error)


def sum_kernel(parts, out):
    total = jnp.sum(parts[...], axis=0)
    for copy in range(out.shape[0]):
        out[copy] = total


def sum_copies(parts, copies):
    return pl.pallas_call(
        sum_kernel,
        out_shape=pltpu.VMEM((copies,) + parts.shape[1:], F32),
        in_specs=[VMEM],
        out_specs=VMEM,
        compiler_params=SMALL,
        name="sum_copies",
    )(parts)


def solve_kernel(replicas, parts, left, out, left_out):
    total = jnp.sum(parts[...], axis=0) * (1.0 / replicas)
    rank, rows = left.shape
    width = out.shape[2]
    table = jnp.concatenate([total[:, width:], left[...], total[:, :width]], axis=1)
    index = lax.broadcasted_iota(jnp.int32, table.shape, 0)
    for step in range(rank):
        scale = lax.rsqrt(table[step : step + 1, step : step + 1])
        pivot = table[step : step + 1, :] * scale
        factor = table[:, step : step + 1] * scale
        table = jnp.where(index > step, table - factor * pivot, jnp.where(index == step, pivot, table))
    left_out[...] = table[:, LANES : LANES + rows]
    for copy in range(out.shape[0]):
        out[copy] = table[:, LANES + rows :]


def solve(parts, left, blocks, replicas):
    _, rank, wide = parts.shape
    return pl.pallas_call(
        functools.partial(solve_kernel, replicas),
        out_shape=(
            pltpu.VMEM((blocks, rank, wide - LANES), F32),
            pltpu.VMEM(left.shape, F32),
        ),
        in_specs=[VMEM, VMEM],
        out_specs=(VMEM, VMEM),
        compiler_params=SMALL,
        name="solve",
    )(parts, left)


def update_kernel(parts, left, update, left_out, right):
    blocks, _, width = parts.shape
    here = 0
    for axis in DP:
        here = here * lax.axis_size(axis) + lax.axis_index(axis)
    update[...] = lax.dot_general(
        left[...], parts[here], (((0,), (0,)), ((), ())), precision=HIGH, preferred_element_type=F32
    )
    left_out[...] = left[...]
    for block in range(blocks):
        right[:, block * width : (block + 1) * width] = parts[block]


def finish(parts, left):
    blocks, rank, width = parts.shape
    return pl.pallas_call(
        update_kernel,
        out_shape=(
            jax.ShapeDtypeStruct((left.shape[1], width), F32),
            jax.ShapeDtypeStruct(left.shape, F32),
            jax.ShapeDtypeStruct((rank, blocks * width), F32),
        ),
        in_specs=[VMEM, VMEM],
        out_specs=(VMEM, VMEM, VMEM),
        compiler_params=SMALL,
        name="update",
    )(parts, left)


def exchange(blocks, axes):
    count = blocks.shape[0]
    order = [(index + FIRST[axes]) % count for index in range(count)]
    return lax.all_to_all(blocks, axes, 0, 0, axis_index_groups=[order])


def on_device(gradient, error_buffer, right_start):
    replicas, blocks, far = (math.prod(lax.axis_size(axis) for axis in axes) for axes in (DP, NEAR, FAR))
    lefts, gradient, error = left_terms(gradient[0], error_buffer[0], right_start, replicas)
    raws, left_sum = raw_terms(exchange(lefts, DP), gradient, error, blocks)
    sums = sum_copies(exchange(raws, NEAR), far)
    rights, left_factor = solve(exchange(sums, FAR), left_sum, blocks, replicas)
    return finish(exchange(rights, NEAR), left_factor)


def solution(mesh):
    split = Mesh(mesh.devices.reshape(4, 2, 4, 4, 2, 2), ("yh", "yl", "x", "zh", "zl", "core"))
    return jax.shard_map(
        on_device,
        mesh=split,
        in_specs=(P(DP, TENSOR, None), P(DP, TENSOR, None), P()),
        out_specs=(P(TENSOR, DP), P(None, TENSOR), P()),
        check_vma=False,
    )
```

```python
import functools
import math

import jax
import jax.numpy as jnp
from jax import lax
from jax.experimental import pallas as pl
from jax.experimental.pallas import tpu as pltpu
from jax.sharding import Mesh
from jax.sharding import PartitionSpec as P

HIGH = lax.Precision.HIGHEST
F32 = jnp.float32
BF16 = jnp.bfloat16
LANES = 128
GAP = 16


def rotated(count, first):
    return [(index + first) % count for index in range(count)]


DP = ("yh", "yl", "x")
TENSOR = ("zh", "zl", "core")
NEAR = ("yl", "zl", "x", "core")
FAR = ("yh", "zh")
ORDERS = {"left": rotated(32, 22), "near": rotated(32, 29), "far": rotated(16, 11), "back": rotated(32, 29)}
VMEM = pl.BlockSpec(memory_space=pltpu.VMEM)
SMALL = pltpu.CompilerParams(vmem_limit_bytes=16 * 2**20)


def pieces(values):
    high = values.astype(BF16).astype(F32)
    rest = values - high
    middle = rest.astype(BF16).astype(F32)
    low = rest - middle
    none = jnp.zeros_like(values)
    return jnp.concatenate([high, middle, low, none], axis=0).astype(BF16)


def fold(products, rank):
    return products[:rank] + (products[rank : 2 * rank] + products[2 * rank : 3 * rank])


def left_kernel(gradient, error, start, out, gradient_here, error_here, start_here, arrived):
    copies = []
    for index, (source, target) in enumerate(((start, start_here), (gradient, gradient_here), (error, error_here))):
        copies.append(pltpu.make_async_copy(source, target, arrived.at[index]))
        copies[-1].start()
    rank = start.shape[0]
    copies[0].wait()
    cut = pieces(start_here[...])
    dims = (((1,), (1,)), ((), ()))
    copies[1].wait()
    total = lax.dot_general(cut, gradient_here[...], dims, preferred_element_type=F32)
    copies[2].wait()
    total += lax.dot_general(cut, error_here[...], dims, preferred_element_type=F32)
    left = fold(total, rank)
    for copy in range(out.shape[0]):
        out[copy] = left


def left_terms(gradient, error, start, replicas):
    rows, columns = gradient.shape
    rank = start.shape[0]
    return pl.pallas_call(
        left_kernel,
        out_shape=(
            pltpu.VMEM((replicas, rank, rows), F32),
            pltpu.VMEM((rows, columns), BF16),
            pltpu.VMEM((rows, columns), BF16),
        ),
        in_specs=[pl.BlockSpec(memory_space=pltpu.HBM)] * 3,
        out_specs=(VMEM, VMEM, VMEM),
        scratch_shapes=[pltpu.VMEM((rank, columns), F32), pltpu.SemaphoreType.DMA((3,))],
        compiler_params=SMALL,
        name="left_terms",
    )(*(pltpu.with_memory_space_constraint(array, pltpu.HBM) for array in (gradient, error, start)))


def raw_kernel(parts, gradient, error, sent, left_out):
    left = jnp.sum(parts[...], axis=0)
    left_out[...] = left
    rank, rows = left.shape
    none = jnp.zeros((GAP - rank, rows), F32)
    filled = jnp.concatenate([left, none] * (LANES // GAP), axis=0)
    gram = lax.dot_general(left, filled, (((1,), (1,)), ((), ())), precision=HIGH, preferred_element_type=F32)
    gram_row = jnp.sum(jnp.where(own_lanes(gram.shape), gram, 0.0), axis=0, keepdims=True)
    cut = pieces(left)
    step = 2 * LANES
    high = rank + 1
    for pair in range(gradient.shape[1] // step):
        span = slice(pair * step, (pair + 1) * step)
        total = jnp.dot(cut, gradient[:, span], preferred_element_type=F32)
        total += jnp.dot(cut, error[:, span], preferred_element_type=F32)
        total = fold(total, rank)
        for half in range(2):
            place = ORDERS["near"].index(ORDERS["back"][2 * pair + half])
            start = place * high
            sent[start : start + rank, :] = total[:, half * LANES : (half + 1) * LANES]
            sent[start + rank : start + high, :] = gram_row


def own_lanes(shape):
    row = lax.broadcasted_iota(jnp.int32, shape, 0)
    lane = lax.broadcasted_iota(jnp.int32, shape, 1)
    return (lane >= row * GAP) & (lane < (row + 1) * GAP)


def raw_terms(parts, gradient, error, blocks):
    _, rank, rows = parts.shape
    return pl.pallas_call(
        raw_kernel,
        out_shape=(
            pltpu.VMEM((blocks * (rank + 1), LANES), F32),
            pltpu.VMEM((rank, rows), F32),
        ),
        in_specs=[VMEM, VMEM, VMEM],
        out_specs=(VMEM, VMEM),
        compiler_params=SMALL,
        name="raw_terms",
    )(parts, gradient, error)


def sum_blocks(parts, count):
    high = parts.shape[0] // count
    terms = [parts[index * high : (index + 1) * high, :] for index in range(count)]
    while len(terms) > 1:
        terms = [one + other for one, other in zip(terms[::2], terms[1::2])]
    return terms[0]


def sum_kernel(count, parts, out):
    total = sum_blocks(parts, count)
    high = total.shape[0]
    for copy in range(out.shape[0] // high):
        out[copy * high : (copy + 1) * high, :] = total


def sum_copies(parts, count, copies):
    high = parts.shape[0] // count
    return pl.pallas_call(
        functools.partial(sum_kernel, count),
        out_shape=pltpu.VMEM((copies * high, LANES), F32),
        in_specs=[VMEM],
        out_specs=VMEM,
        compiler_params=SMALL,
        name="sum_copies",
    )(parts)


def solve_kernel(replicas, count, parts, left, out, left_out):
    total = sum_blocks(parts, count) * (1.0 / replicas)
    rank, rows = left.shape
    gram = jnp.broadcast_to(total[rank:], (rank, LANES))
    gram = jnp.where(own_lanes(gram.shape), gram, 0.0)
    shift = LANES // 2
    while shift >= GAP:
        gram = gram + pltpu.roll(gram, shift, 1)
        shift //= 2
    table = jnp.concatenate([gram, left[...], total[:rank]], axis=1)
    index = lax.broadcasted_iota(jnp.int32, table.shape, 0)
    for step in range(rank):
        scale = lax.rsqrt(table[step : step + 1, step : step + 1])
        pivot = table[step : step + 1, :] * scale
        factor = table[:, step : step + 1] * scale
        table = jnp.where(index > step, table - factor * pivot, jnp.where(index == step, pivot, table))
    left_out[...] = table[:, LANES : LANES + rows]
    for copy in range(out.shape[0]):
        out[copy] = table[:, LANES + rows :]


def solve(parts, count, left, blocks, replicas):
    rank = left.shape[0]
    return pl.pallas_call(
        functools.partial(solve_kernel, replicas, count),
        out_shape=(
            pltpu.VMEM((blocks, rank, LANES), F32),
            pltpu.VMEM(left.shape, F32),
        ),
        in_specs=[VMEM, VMEM],
        out_specs=(VMEM, VMEM),
        compiler_params=SMALL,
        name="solve",
    )(parts, left)


def update_kernel(parts, left, update, left_out, right):
    blocks, _, width = parts.shape
    here = 0
    for axis in DP:
        here = here * lax.axis_size(axis) + lax.axis_index(axis)
    update[...] = lax.dot_general(
        left[...], parts[here], (((0,), (0,)), ((), ())), precision=HIGH, preferred_element_type=F32
    )
    left_out[...] = left[...]
    for block in range(blocks):
        right[:, block * width : (block + 1) * width] = parts[block]


def finish(parts, left):
    blocks, rank, width = parts.shape
    return pl.pallas_call(
        update_kernel,
        out_shape=(
            jax.ShapeDtypeStruct((left.shape[1], width), F32),
            jax.ShapeDtypeStruct(left.shape, F32),
            jax.ShapeDtypeStruct((rank, blocks * width), F32),
        ),
        in_specs=[VMEM, VMEM],
        out_specs=(VMEM, VMEM, VMEM),
        compiler_params=SMALL,
        name="update",
    )(parts, left)


def exchange(blocks, axes, order):
    return lax.all_to_all(blocks, axes, 0, 0, axis_index_groups=[ORDERS[order]])


def exchange_rows(rows, axes, order):
    count = len(ORDERS[order])
    high = rows.shape[0] // count
    return exchange(rows.reshape(count, high, 1, LANES), axes, order).reshape(rows.shape)


def on_device(gradient, error_buffer, right_start):
    replicas, blocks, far = (math.prod(lax.axis_size(axis) for axis in axes) for axes in (DP, NEAR, FAR))
    lefts, gradient, error = left_terms(gradient[0], error_buffer[0], right_start, replicas)
    raws, left_sum = raw_terms(exchange(lefts, DP, "left"), gradient, error, blocks)
    sums = sum_copies(exchange_rows(raws, NEAR, "near"), blocks, far)
    rights, left_factor = solve(exchange_rows(sums, FAR, "far"), far, left_sum, blocks, replicas)
    return finish(exchange(rights, NEAR, "back"), left_factor)


def solution(mesh):
    split = Mesh(mesh.devices.reshape(4, 2, 4, 4, 2, 2), ("yh", "yl", "x", "zh", "zl", "core"))
    return jax.shard_map(
        on_device,
        mesh=split,
        in_specs=(P(DP, TENSOR, None), P(DP, TENSOR, None), P()),
        out_specs=(P(TENSOR, DP), P(None, TENSOR), P()),
        check_vma=False,
    )
```

```python
import functools
import math

import jax
import jax.numpy as jnp
from jax import lax
from jax.experimental import pallas as pl
from jax.experimental.pallas import tpu as pltpu
from jax.sharding import Mesh
from jax.sharding import PartitionSpec as P

HIGH = lax.Precision.HIGHEST
F32 = jnp.float32
BF16 = jnp.bfloat16
LANES = 128
GAP = 16


def rotated(count, first):
    return [(index + first) % count for index in range(count)]


DP = ("yh", "yl", "x")
TENSOR = ("zh", "zl", "core")
NEAR = ("yl", "zl", "x", "core")
FAR = ("yh", "zh")
ORDERS = {"left": rotated(32, 22), "near": rotated(32, 29), "far": rotated(16, 11), "back": rotated(32, 29)}
VMEM = pl.BlockSpec(memory_space=pltpu.VMEM)
SMALL = pltpu.CompilerParams(vmem_limit_bytes=16 * 2**20)


def pieces(values):
    high = values.astype(BF16).astype(F32)
    rest = values - high
    middle = rest.astype(BF16).astype(F32)
    low = rest - middle
    none = jnp.zeros_like(values)
    return jnp.concatenate([high, middle, low, none], axis=0).astype(BF16)


def fold(products, rank):
    return products[:rank] + (products[rank : 2 * rank] + products[2 * rank : 3 * rank])


def left_kernel(gradient, error, start, out, gradient_here, error_here, start_here, arrived):
    first = pltpu.make_async_copy(start, start_here, arrived.at[0])
    first.start()
    columns = gradient.shape[1]
    edges = [0, columns // 4, columns * 5 // 8, columns]
    spans = list(zip(edges[:-1], edges[1:]))
    copies = []
    for index, (low, high) in enumerate(spans):
        pair = []
        for which, (source, target) in enumerate(((gradient, gradient_here), (error, error_here))):
            span = pl.ds(low, high - low)
            copy = pltpu.make_async_copy(source.at[:, span], target.at[:, span], arrived.at[1 + 2 * index + which])
            copy.start()
            pair.append(copy)
        copies.append(pair)
    first.wait()
    cut = pieces(start_here[...]).astype(F32).T.astype(BF16)
    total = 0.0
    for (low, high), pair in zip(spans, copies):
        for copy in pair:
            copy.wait()
        total += jnp.dot(gradient_here[:, low:high], cut[low:high], preferred_element_type=F32) + jnp.dot(
            error_here[:, low:high], cut[low:high], preferred_element_type=F32
        )
    left = fold(total.T, start.shape[0])
    for copy in range(out.shape[0]):
        out[copy] = left


def left_terms(gradient, error, start, replicas):
    rows, columns = gradient.shape
    rank = start.shape[0]
    return pl.pallas_call(
        left_kernel,
        out_shape=(
            pltpu.VMEM((replicas, rank, rows), F32),
            pltpu.VMEM((rows, columns), BF16),
            pltpu.VMEM((rows, columns), BF16),
        ),
        in_specs=[pl.BlockSpec(memory_space=pltpu.HBM)] * 3,
        out_specs=(VMEM, VMEM, VMEM),
        scratch_shapes=[pltpu.VMEM((rank, columns), F32), pltpu.SemaphoreType.DMA((7,))],
        compiler_params=SMALL,
        name="left_terms",
    )(*(pltpu.with_memory_space_constraint(array, pltpu.HBM) for array in (gradient, error, start)))


def raw_kernel(parts, gradient, error, sent, left_out):
    left = jnp.sum(parts[...], axis=0)
    left_out[...] = left
    rank, rows = left.shape
    none = jnp.zeros((GAP - rank, rows), F32)
    filled = jnp.concatenate([left, none] * (LANES // GAP), axis=0)
    gram = lax.dot_general(left, filled, (((1,), (1,)), ((), ())), precision=HIGH, preferred_element_type=F32)
    gram_row = jnp.sum(jnp.where(own_lanes(gram.shape), gram, 0.0), axis=0, keepdims=True)
    cut = pieces(left)
    step = 2 * LANES
    high = rank + 1
    for pair in range(gradient.shape[1] // step):
        span = slice(pair * step, (pair + 1) * step)
        total = jnp.dot(cut, gradient[:, span], preferred_element_type=F32)
        total += jnp.dot(cut, error[:, span], preferred_element_type=F32)
        total = fold(total, rank)
        for half in range(2):
            place = ORDERS["near"].index(ORDERS["back"][2 * pair + half])
            start = place * high
            sent[start : start + rank, :] = total[:, half * LANES : (half + 1) * LANES]
            sent[start + rank : start + high, :] = gram_row


def own_lanes(shape):
    row = lax.broadcasted_iota(jnp.int32, shape, 0)
    lane = lax.broadcasted_iota(jnp.int32, shape, 1)
    return (lane >= row * GAP) & (lane < (row + 1) * GAP)


def raw_terms(parts, gradient, error, blocks):
    _, rank, rows = parts.shape
    return pl.pallas_call(
        raw_kernel,
        out_shape=(
            pltpu.VMEM((blocks * (rank + 1), LANES), F32),
            pltpu.VMEM((rank, rows), F32),
        ),
        in_specs=[VMEM, VMEM, VMEM],
        out_specs=(VMEM, VMEM),
        compiler_params=SMALL,
        name="raw_terms",
    )(parts, gradient, error)


def sum_blocks(parts, count):
    high = parts.shape[0] // count
    terms = [parts[index * high : (index + 1) * high, :] for index in range(count)]
    while len(terms) > 1:
        terms = [one + other for one, other in zip(terms[::2], terms[1::2])]
    return terms[0]


def sum_kernel(count, parts, out):
    total = sum_blocks(parts, count)
    high = total.shape[0]
    for copy in range(out.shape[0] // high):
        out[copy * high : (copy + 1) * high, :] = total


def sum_copies(parts, count, copies):
    high = parts.shape[0] // count
    return pl.pallas_call(
        functools.partial(sum_kernel, count),
        out_shape=pltpu.VMEM((copies * high, LANES), F32),
        in_specs=[VMEM],
        out_specs=VMEM,
        compiler_params=SMALL,
        name="sum_copies",
    )(parts)


def solve_kernel(replicas, count, parts, left, out, left_out):
    total = sum_blocks(parts, count) * (1.0 / replicas)
    rank, rows = left.shape
    gram = jnp.broadcast_to(total[rank:], (rank, LANES))
    gram = jnp.where(own_lanes(gram.shape), gram, 0.0)
    shift = LANES // 2
    while shift >= GAP:
        gram = gram + pltpu.roll(gram, shift, 1)
        shift //= 2
    spread = [jnp.broadcast_to(gram[:, column : column + 1], (rank, LANES)) for column in range(rank)]
    values = [left[:, low : low + LANES] for low in range(0, rows, LANES)] + [total[:rank]]
    index = lax.broadcasted_iota(jnp.int32, (rank, LANES), 0)
    for step in range(rank):
        scale = lax.rsqrt(spread[step][step : step + 1, :])
        factor = spread[step] * scale

        def eliminate(table):
            pivot = table[step : step + 1, :] * scale
            return jnp.where(index > step, table - factor * pivot, jnp.where(index == step, pivot, table))

        spread = spread[: step + 1] + [eliminate(table) for table in spread[step + 1 :]]
        values = [eliminate(table) for table in values]
    for place, low in enumerate(range(0, rows, LANES)):
        left_out[:, low : low + LANES] = values[place]
    for copy in range(out.shape[0]):
        out[copy] = values[-1]


def solve(parts, count, left, blocks, replicas):
    rank = left.shape[0]
    return pl.pallas_call(
        functools.partial(solve_kernel, replicas, count),
        out_shape=(
            pltpu.VMEM((blocks, rank, LANES), F32),
            pltpu.VMEM(left.shape, F32),
        ),
        in_specs=[VMEM, VMEM],
        out_specs=(VMEM, VMEM),
        compiler_params=SMALL,
        name="solve",
    )(parts, left)


def update_kernel(parts, left, update, left_out, right):
    blocks, _, width = parts.shape
    here = 0
    for axis in DP:
        here = here * lax.axis_size(axis) + lax.axis_index(axis)
    update[...] = lax.dot_general(
        left[...], parts[here], (((0,), (0,)), ((), ())), precision=HIGH, preferred_element_type=F32
    )
    left_out[...] = left[...]
    for block in range(blocks):
        right[:, block * width : (block + 1) * width] = parts[block]


def finish(parts, left):
    blocks, rank, width = parts.shape
    return pl.pallas_call(
        update_kernel,
        out_shape=(
            jax.ShapeDtypeStruct((left.shape[1], width), F32),
            jax.ShapeDtypeStruct(left.shape, F32),
            jax.ShapeDtypeStruct((rank, blocks * width), F32),
        ),
        in_specs=[VMEM, VMEM],
        out_specs=(VMEM, VMEM, VMEM),
        compiler_params=SMALL,
        name="update",
    )(parts, left)


def exchange(blocks, axes, order):
    return lax.all_to_all(blocks, axes, 0, 0, axis_index_groups=[ORDERS[order]])


def exchange_rows(rows, axes, order):
    count = len(ORDERS[order])
    high = rows.shape[0] // count
    return exchange(rows.reshape(count, high, 1, LANES), axes, order).reshape(rows.shape)


def on_device(gradient, error_buffer, right_start):
    replicas, blocks, far = (math.prod(lax.axis_size(axis) for axis in axes) for axes in (DP, NEAR, FAR))
    lefts, gradient, error = left_terms(gradient[0], error_buffer[0], right_start, replicas)
    raws, left_sum = raw_terms(exchange(lefts, DP, "left"), gradient, error, blocks)
    sums = sum_copies(exchange_rows(raws, NEAR, "near"), blocks, far)
    rights, left_factor = solve(exchange_rows(sums, FAR, "far"), far, left_sum, blocks, replicas)
    return finish(exchange(rights, NEAR, "back"), left_factor)


def solution(mesh):
    split = Mesh(mesh.devices.reshape(4, 2, 4, 4, 2, 2), ("yh", "yl", "x", "zh", "zl", "core"))
    return jax.shard_map(
        on_device,
        mesh=split,
        in_specs=(P(DP, TENSOR, None), P(DP, TENSOR, None), P()),
        out_specs=(P(TENSOR, DP), P(None, TENSOR), P()),
        check_vma=False,
    )
```

```python
import functools
import math

import jax
import jax.numpy as jnp
from jax import lax
from jax.experimental import pallas as pl
from jax.experimental.pallas import tpu as pltpu
from jax.sharding import Mesh
from jax.sharding import PartitionSpec as P

HIGH = lax.Precision.HIGHEST
F32 = jnp.float32
BF16 = jnp.bfloat16
LANES = 128
GAP = 16


def rotated(count, first):
    return [(index + first) % count for index in range(count)]


DP = ("yh", "yl", "x")
TENSOR = ("zh", "zl", "core")
NEAR = ("yl", "zl", "x", "core")
FAR = ("yh", "zh")
ORDERS = {"left": rotated(32, 22), "near": rotated(32, 29), "far": rotated(16, 11), "back": rotated(32, 29)}
VMEM = pl.BlockSpec(memory_space=pltpu.VMEM)
SMALL = pltpu.CompilerParams(vmem_limit_bytes=16 * 2**20)


def pieces(values):
    high = values.astype(BF16).astype(F32)
    rest = values - high
    middle = rest.astype(BF16).astype(F32)
    low = rest - middle
    none = jnp.zeros_like(values)
    return jnp.concatenate([high, middle, low, none], axis=0).astype(BF16)


def stacked(one, other, axis):
    cuts = []
    for values in (one, other):
        high = values.astype(BF16).astype(F32)
        middle = (values - high).astype(BF16).astype(F32)
        cuts.append((high, middle, values - high - middle))
    (high, middle, low), (high2, middle2, low2) = cuts
    first = jnp.concatenate([high, high, middle, high, low, middle], axis=axis)
    second = jnp.concatenate([high2, middle2, high2, low2, high2, middle2], axis=axis)
    return first.astype(BF16), second.astype(BF16)


def fold(products, rank):
    return products[:rank] + (products[rank : 2 * rank] + products[2 * rank : 3 * rank])


def left_kernel(gradient, error, start, out, gradient_here, error_here, start_here, arrived):
    first = pltpu.make_async_copy(start, start_here, arrived.at[0])
    first.start()
    columns = gradient.shape[1]
    edges = [0, columns // 4, columns * 5 // 8, columns]
    spans = list(zip(edges[:-1], edges[1:]))
    copies = []
    for index, (low, high) in enumerate(spans):
        pair = []
        for which, (source, target) in enumerate(((gradient, gradient_here), (error, error_here))):
            span = pl.ds(low, high - low)
            copy = pltpu.make_async_copy(source.at[:, span], target.at[:, span], arrived.at[1 + 2 * index + which])
            copy.start()
            pair.append(copy)
        copies.append(pair)
    first.wait()
    cut = pieces(start_here[...]).astype(F32).T.astype(BF16)
    total = 0.0
    for (low, high), pair in zip(spans, copies):
        for copy in pair:
            copy.wait()
        total += jnp.dot(gradient_here[:, low:high], cut[low:high], preferred_element_type=F32) + jnp.dot(
            error_here[:, low:high], cut[low:high], preferred_element_type=F32
        )
    left = fold(total.T, start.shape[0])
    for copy in range(out.shape[0]):
        out[copy] = left


def left_terms(gradient, error, start, replicas):
    rows, columns = gradient.shape
    rank = start.shape[0]
    return pl.pallas_call(
        left_kernel,
        out_shape=(
            pltpu.VMEM((replicas, rank, rows), F32),
            pltpu.VMEM((rows, columns), BF16),
            pltpu.VMEM((rows, columns), BF16),
        ),
        in_specs=[pl.BlockSpec(memory_space=pltpu.HBM)] * 3,
        out_specs=(VMEM, VMEM, VMEM),
        scratch_shapes=[pltpu.VMEM((rank, columns), F32), pltpu.SemaphoreType.DMA((7,))],
        compiler_params=SMALL,
        name="left_terms",
    )(*(pltpu.with_memory_space_constraint(array, pltpu.HBM) for array in (gradient, error, start)))


def raw_kernel(parts, gradient, error, sent, left_out):
    left = jnp.sum(parts[...], axis=0)
    left_out[...] = left
    rank, rows = left.shape
    none = jnp.zeros((GAP - rank, rows), F32)
    filled = jnp.concatenate([left, none] * (LANES // GAP), axis=0)
    gram = lax.dot_general(left, filled, (((1,), (1,)), ((), ())), precision=HIGH, preferred_element_type=F32)
    gram_row = jnp.sum(jnp.where(own_lanes(gram.shape), gram, 0.0), axis=0, keepdims=True)
    cut = pieces(left)
    step = 2 * LANES
    high = rank + 1
    for pair in range(gradient.shape[1] // step):
        span = slice(pair * step, (pair + 1) * step)
        total = jnp.dot(cut, gradient[:, span], preferred_element_type=F32)
        total += jnp.dot(cut, error[:, span], preferred_element_type=F32)
        total = fold(total, rank)
        for half in range(2):
            place = ORDERS["near"].index(ORDERS["back"][2 * pair + half])
            start = place * high
            sent[start : start + rank, :] = total[:, half * LANES : (half + 1) * LANES]
            sent[start + rank : start + high, :] = gram_row


def own_lanes(shape):
    row = lax.broadcasted_iota(jnp.int32, shape, 0)
    lane = lax.broadcasted_iota(jnp.int32, shape, 1)
    return (lane >= row * GAP) & (lane < (row + 1) * GAP)


def raw_terms(parts, gradient, error, blocks):
    _, rank, rows = parts.shape
    return pl.pallas_call(
        raw_kernel,
        out_shape=(
            pltpu.VMEM((blocks * (rank + 1), LANES), F32),
            pltpu.VMEM((rank, rows), F32),
        ),
        in_specs=[VMEM, VMEM, VMEM],
        out_specs=(VMEM, VMEM),
        compiler_params=SMALL,
        name="raw_terms",
    )(parts, gradient, error)


def sum_blocks(parts, count):
    high = parts.shape[0] // count
    terms = [parts[index * high : (index + 1) * high, :] for index in range(count)]
    while len(terms) > 1:
        terms = [one + other for one, other in zip(terms[::2], terms[1::2])]
    return terms[0]


def sum_kernel(count, parts, out):
    total = sum_blocks(parts, count)
    high = total.shape[0]
    for copy in range(out.shape[0] // high):
        out[copy * high : (copy + 1) * high, :] = total


def sum_copies(parts, count, copies):
    high = parts.shape[0] // count
    return pl.pallas_call(
        functools.partial(sum_kernel, count),
        out_shape=pltpu.VMEM((copies * high, LANES), F32),
        in_specs=[VMEM],
        out_specs=VMEM,
        compiler_params=SMALL,
        name="sum_copies",
    )(parts)


def solve_kernel(replicas, count, parts, left, out, left_out):
    total = sum_blocks(parts, count) * (1.0 / replicas)
    rank, rows = left.shape
    gram = jnp.broadcast_to(total[rank:], (rank, LANES))
    gram = jnp.where(own_lanes(gram.shape), gram, 0.0)
    shift = LANES // 2
    while shift >= GAP:
        gram = gram + pltpu.roll(gram, shift, 1)
        shift //= 2
    spread = [jnp.broadcast_to(gram[:, column : column + 1], (rank, LANES)) for column in range(rank)]
    values = [left[:, low : low + LANES] for low in range(0, rows, LANES)] + [total[:rank]]
    index = lax.broadcasted_iota(jnp.int32, (rank, LANES), 0)
    for step in range(rank):
        scale = lax.rsqrt(spread[step][step : step + 1, :])
        factor = spread[step] * scale

        def eliminate(table):
            pivot = table[step : step + 1, :] * scale
            return jnp.where(index > step, table - factor * pivot, jnp.where(index == step, pivot, table))

        spread = spread[: step + 1] + [eliminate(table) for table in spread[step + 1 :]]
        values = [eliminate(table) for table in values]
    for place, low in enumerate(range(0, rows, LANES)):
        left_out[:, low : low + LANES] = values[place]
    for copy in range(out.shape[0]):
        out[copy] = values[-1]


def solve(parts, count, left, blocks, replicas):
    rank = left.shape[0]
    return pl.pallas_call(
        functools.partial(solve_kernel, replicas, count),
        out_shape=(
            pltpu.VMEM((blocks, rank, LANES), F32),
            pltpu.VMEM(left.shape, F32),
        ),
        in_specs=[VMEM, VMEM],
        out_specs=(VMEM, VMEM),
        compiler_params=SMALL,
        name="solve",
    )(parts, left)


def update_kernel(parts, left, update, left_out, right):
    blocks, _, width = parts.shape
    here = 0
    for axis in DP:
        here = here * lax.axis_size(axis) + lax.axis_index(axis)
    first, second = stacked(left[...], parts[here], 0)
    update[...] = lax.dot_general(first, second, (((0,), (0,)), ((), ())), preferred_element_type=F32)
    left_out[...] = left[...]
    for block in range(blocks):
        right[:, block * width : (block + 1) * width] = parts[block]


def finish(parts, left):
    blocks, rank, width = parts.shape
    return pl.pallas_call(
        update_kernel,
        out_shape=(
            jax.ShapeDtypeStruct((left.shape[1], width), F32),
            jax.ShapeDtypeStruct(left.shape, F32),
            jax.ShapeDtypeStruct((rank, blocks * width), F32),
        ),
        in_specs=[VMEM, VMEM],
        out_specs=(VMEM, VMEM, VMEM),
        compiler_params=SMALL,
        name="update",
    )(parts, left)


def exchange(blocks, axes, order):
    return lax.all_to_all(blocks, axes, 0, 0, axis_index_groups=[ORDERS[order]])


def exchange_rows(rows, axes, order):
    count = len(ORDERS[order])
    high = rows.shape[0] // count
    return exchange(rows.reshape(count, high, 1, LANES), axes, order).reshape(rows.shape)


def on_device(gradient, error_buffer, right_start):
    replicas, blocks, far = (math.prod(lax.axis_size(axis) for axis in axes) for axes in (DP, NEAR, FAR))
    lefts, gradient, error = left_terms(gradient[0], error_buffer[0], right_start, replicas)
    raws, left_sum = raw_terms(exchange(lefts, DP, "left"), gradient, error, blocks)
    sums = sum_copies(exchange_rows(raws, NEAR, "near"), blocks, far)
    rights, left_factor = solve(exchange_rows(sums, FAR, "far"), far, left_sum, blocks, replicas)
    return finish(exchange(rights, NEAR, "back"), left_factor)


def solution(mesh):
    split = Mesh(mesh.devices.reshape(4, 2, 4, 4, 2, 2), ("yh", "yl", "x", "zh", "zl", "core"))
    return jax.shard_map(
        on_device,
        mesh=split,
        in_specs=(P(DP, TENSOR, None), P(DP, TENSOR, None), P()),
        out_specs=(P(TENSOR, DP), P(None, TENSOR), P()),
        check_vma=False,
    )
```

```python
import functools
import itertools
import math

import jax
import jax.numpy as jnp
from jax import lax
from jax.experimental import pallas as pl
from jax.experimental.pallas import tpu as pltpu
from jax.sharding import Mesh
from jax.sharding import PartitionSpec as P

HIGH = lax.Precision.HIGHEST
F32 = jnp.float32
BF16 = jnp.bfloat16
LANES = 128
GAP = 16


def rotated(count, first):
    return [(index + first) % count for index in range(count)]


DP = ("yh", "yl", "x")
TENSOR = ("zh", "zl", "core")
NEAR = ("yl", "zl", "x", "core")
FAR = ("yh", "zh")
ALL = ("yh", "yl", "x", "zh", "zl", "core")
def far_groups(even, odd):
    groups = []
    for yl, x, zl, core in itertools.product(range(2), range(4), range(2), range(2)):
        order = rotated(16, odd if zl else even)
        groups.append([((((place // 4 * 2 + yl) * 4 + x) * 4 + place % 4) * 2 + zl) * 2 + core for place in order])
    return groups


ORDERS = {"left": rotated(32, 22), "near": rotated(32, 29), "far": far_groups(11, 10), "back": rotated(32, 29)}
VMEM = pl.BlockSpec(memory_space=pltpu.VMEM)
SMALL = pltpu.CompilerParams(vmem_limit_bytes=16 * 2**20)


def pieces(values):
    high = values.astype(BF16).astype(F32)
    rest = values - high
    middle = rest.astype(BF16).astype(F32)
    low = rest - middle
    none = jnp.zeros_like(values)
    return jnp.concatenate([high, middle, low, none], axis=0).astype(BF16)


def stacked(one, other, axis):
    cuts = []
    for values in (one, other):
        high = values.astype(BF16).astype(F32)
        middle = (values - high).astype(BF16).astype(F32)
        cuts.append((high, middle, values - high - middle))
    (high, middle, low), (high2, middle2, low2) = cuts
    first = jnp.concatenate([high, high, middle, high, low, middle], axis=axis)
    second = jnp.concatenate([high2, middle2, high2, low2, high2, middle2], axis=axis)
    return first.astype(BF16), second.astype(BF16)


def fold(products, rank):
    return products[:rank] + (products[rank : 2 * rank] + products[2 * rank : 3 * rank])


def left_kernel(gradient, error, start, out, gradient_here, error_here, start_here, arrived):
    first = pltpu.make_async_copy(start, start_here, arrived.at[0])
    first.start()
    columns = gradient.shape[1]
    edges = [0, columns // 4, columns * 5 // 8, columns]
    spans = list(zip(edges[:-1], edges[1:]))
    copies = []
    for index, (low, high) in enumerate(spans):
        pair = []
        for which, (source, target) in enumerate(((gradient, gradient_here), (error, error_here))):
            span = pl.ds(low, high - low)
            copy = pltpu.make_async_copy(source.at[:, span], target.at[:, span], arrived.at[1 + 2 * index + which])
            copy.start()
            pair.append(copy)
        copies.append(pair)
    first.wait()
    cut = pieces(start_here[...]).astype(F32).T.astype(BF16)
    total = 0.0
    for (low, high), pair in zip(spans, copies):
        for copy in pair:
            copy.wait()
        total += jnp.dot(gradient_here[:, low:high], cut[low:high], preferred_element_type=F32) + jnp.dot(
            error_here[:, low:high], cut[low:high], preferred_element_type=F32
        )
    left = fold(total.T, start.shape[0])
    for copy in range(out.shape[0]):
        out[copy] = left


def left_terms(gradient, error, start, replicas):
    rows, columns = gradient.shape
    rank = start.shape[0]
    return pl.pallas_call(
        left_kernel,
        out_shape=(
            pltpu.VMEM((replicas, rank, rows), F32),
            pltpu.VMEM((rows, columns), BF16),
            pltpu.VMEM((rows, columns), BF16),
        ),
        in_specs=[pl.BlockSpec(memory_space=pltpu.HBM)] * 3,
        out_specs=(VMEM, VMEM, VMEM),
        scratch_shapes=[pltpu.VMEM((rank, columns), F32), pltpu.SemaphoreType.DMA((7,))],
        compiler_params=SMALL,
        name="left_terms",
    )(*(pltpu.with_memory_space_constraint(array, pltpu.HBM) for array in (gradient, error, start)))


def raw_kernel(parts, gradient, error, sent, left_out):
    left = jnp.sum(parts[...], axis=0)
    left_out[...] = left
    rank, rows = left.shape
    none = jnp.zeros((GAP - rank, rows), F32)
    filled = jnp.concatenate([left, none] * (LANES // GAP), axis=0)
    gram = lax.dot_general(left, filled, (((1,), (1,)), ((), ())), precision=HIGH, preferred_element_type=F32)
    gram_row = jnp.sum(jnp.where(own_lanes(gram.shape), gram, 0.0), axis=0, keepdims=True)
    cut = pieces(left)
    step = 2 * LANES
    high = rank + 1
    for pair in range(gradient.shape[1] // step):
        span = slice(pair * step, (pair + 1) * step)
        total = jnp.dot(cut, gradient[:, span], preferred_element_type=F32)
        total += jnp.dot(cut, error[:, span], preferred_element_type=F32)
        total = fold(total, rank)
        for half in range(2):
            place = ORDERS["near"].index(ORDERS["back"][2 * pair + half])
            start = place * high
            sent[start : start + rank, :] = total[:, half * LANES : (half + 1) * LANES]
            sent[start + rank : start + high, :] = gram_row


def own_lanes(shape):
    row = lax.broadcasted_iota(jnp.int32, shape, 0)
    lane = lax.broadcasted_iota(jnp.int32, shape, 1)
    return (lane >= row * GAP) & (lane < (row + 1) * GAP)


def raw_terms(parts, gradient, error, blocks):
    _, rank, rows = parts.shape
    return pl.pallas_call(
        raw_kernel,
        out_shape=(
            pltpu.VMEM((blocks * (rank + 1), LANES), F32),
            pltpu.VMEM((rank, rows), F32),
        ),
        in_specs=[VMEM, VMEM, VMEM],
        out_specs=(VMEM, VMEM),
        compiler_params=SMALL,
        name="raw_terms",
    )(parts, gradient, error)


def sum_blocks(parts, count):
    high = parts.shape[0] // count
    terms = [parts[index * high : (index + 1) * high, :] for index in range(count)]
    while len(terms) > 1:
        terms = [one + other for one, other in zip(terms[::2], terms[1::2])]
    return terms[0]


def sum_kernel(count, parts, out):
    total = sum_blocks(parts, count)
    high = total.shape[0]
    for copy in range(out.shape[0] // high):
        out[copy * high : (copy + 1) * high, :] = total


def sum_copies(parts, count, copies):
    high = parts.shape[0] // count
    return pl.pallas_call(
        functools.partial(sum_kernel, count),
        out_shape=pltpu.VMEM((copies * high, LANES), F32),
        in_specs=[VMEM],
        out_specs=VMEM,
        compiler_params=SMALL,
        name="sum_copies",
    )(parts)


def solve_kernel(replicas, count, parts, left, out, left_out):
    total = sum_blocks(parts, count) * (1.0 / replicas)
    rank, rows = left.shape
    gram = jnp.broadcast_to(total[rank:], (rank, LANES))
    gram = jnp.where(own_lanes(gram.shape), gram, 0.0)
    shift = LANES // 2
    while shift >= GAP:
        gram = gram + pltpu.roll(gram, shift, 1)
        shift //= 2
    spread = [jnp.broadcast_to(gram[:, column : column + 1], (rank, LANES)) for column in range(rank)]
    values = [left[:, low : low + LANES] for low in range(0, rows, LANES)] + [total[:rank]]
    index = lax.broadcasted_iota(jnp.int32, (rank, LANES), 0)
    for step in range(rank):
        scale = lax.rsqrt(spread[step][step : step + 1, :])
        factor = spread[step] * scale

        def eliminate(table):
            pivot = table[step : step + 1, :] * scale
            return jnp.where(index > step, table - factor * pivot, jnp.where(index == step, pivot, table))

        spread = spread[: step + 1] + [eliminate(table) for table in spread[step + 1 :]]
        values = [eliminate(table) for table in values]
    for place, low in enumerate(range(0, rows, LANES)):
        left_out[:, low : low + LANES] = values[place]
    for copy in range(out.shape[0]):
        out[copy] = values[-1]


def solve(parts, count, left, blocks, replicas):
    rank = left.shape[0]
    return pl.pallas_call(
        functools.partial(solve_kernel, replicas, count),
        out_shape=(
            pltpu.VMEM((blocks, rank, LANES), F32),
            pltpu.VMEM(left.shape, F32),
        ),
        in_specs=[VMEM, VMEM],
        out_specs=(VMEM, VMEM),
        compiler_params=SMALL,
        name="solve",
    )(parts, left)


def update_kernel(parts, left, update, left_out, right):
    blocks, _, width = parts.shape
    here = 0
    for axis in DP:
        here = here * lax.axis_size(axis) + lax.axis_index(axis)
    first, second = stacked(left[...], parts[here], 0)
    update[...] = lax.dot_general(first, second, (((0,), (0,)), ((), ())), preferred_element_type=F32)
    left_out[...] = left[...]
    for block in range(blocks):
        right[:, block * width : (block + 1) * width] = parts[block]


def finish(parts, left):
    blocks, rank, width = parts.shape
    return pl.pallas_call(
        update_kernel,
        out_shape=(
            jax.ShapeDtypeStruct((left.shape[1], width), F32),
            jax.ShapeDtypeStruct(left.shape, F32),
            jax.ShapeDtypeStruct((rank, blocks * width), F32),
        ),
        in_specs=[VMEM, VMEM],
        out_specs=(VMEM, VMEM, VMEM),
        compiler_params=SMALL,
        name="update",
    )(parts, left)


def exchange(blocks, axes, order):
    if order == "far":
        return lax.all_to_all(blocks, ALL, 0, 0, axis_index_groups=ORDERS[order])
    return lax.all_to_all(blocks, axes, 0, 0, axis_index_groups=[ORDERS[order]])


def exchange_rows(rows, axes, order):
    count = math.prod(lax.axis_size(axis) for axis in axes)
    high = rows.shape[0] // count
    return exchange(rows.reshape(count, high, 1, LANES), axes, order).reshape(rows.shape)


def on_device(gradient, error_buffer, right_start):
    replicas, blocks, far = (math.prod(lax.axis_size(axis) for axis in axes) for axes in (DP, NEAR, FAR))
    lefts, gradient, error = left_terms(gradient[0], error_buffer[0], right_start, replicas)
    raws, left_sum = raw_terms(exchange(lefts, DP, "left"), gradient, error, blocks)
    sums = sum_copies(exchange_rows(raws, NEAR, "near"), blocks, far)
    rights, left_factor = solve(exchange_rows(sums, FAR, "far"), far, left_sum, blocks, replicas)
    return finish(exchange(rights, NEAR, "back"), left_factor)


def solution(mesh):
    split = Mesh(mesh.devices.reshape(4, 2, 4, 4, 2, 2), ("yh", "yl", "x", "zh", "zl", "core"))
    return jax.shard_map(
        on_device,
        mesh=split,
        in_specs=(P(DP, TENSOR, None), P(DP, TENSOR, None), P()),
        out_specs=(P(TENSOR, DP), P(None, TENSOR), P()),
        check_vma=False,
    )
```

```python
import functools
import itertools
import math

import jax
import jax.numpy as jnp
from jax import lax
from jax.experimental import pallas as pl
from jax.experimental.pallas import tpu as pltpu
from jax.sharding import Mesh
from jax.sharding import PartitionSpec as P

HIGH = lax.Precision.HIGHEST
F32 = jnp.float32
BF16 = jnp.bfloat16
LANES = 128
GAP = 16


def rotated(count, first):
    return [(index + first) % count for index in range(count)]


DP = ("yh", "yl", "x")
TENSOR = ("zh", "zl", "core")
NEAR = ("yl", "zl", "x", "core")
FAR = ("yh", "zh")
ALL = ("yh", "yl", "x", "zh", "zl", "core")
def far_groups(even, odd):
    groups = []
    for yl, x, zl, core in itertools.product(range(2), range(4), range(2), range(2)):
        order = rotated(16, odd if zl else even)
        groups.append([((((place // 4 * 2 + yl) * 4 + x) * 4 + place % 4) * 2 + zl) * 2 + core for place in order])
    return groups


ORDERS = {"left": rotated(32, 18), "near": rotated(32, 29), "far": far_groups(11, 10), "back": rotated(32, 29)}
VMEM = pl.BlockSpec(memory_space=pltpu.VMEM)
SMALL = pltpu.CompilerParams(vmem_limit_bytes=16 * 2**20)


def pieces(values):
    high = values.astype(BF16).astype(F32)
    rest = values - high
    middle = rest.astype(BF16).astype(F32)
    low = rest - middle
    none = jnp.zeros_like(values)
    return jnp.concatenate([high, middle, low, none], axis=0).astype(BF16)


def stacked(one, other, axis):
    cuts = []
    for values in (one, other):
        high = values.astype(BF16).astype(F32)
        middle = (values - high).astype(BF16).astype(F32)
        cuts.append((high, middle, values - high - middle))
    (high, middle, low), (high2, middle2, low2) = cuts
    first = jnp.concatenate([high, high, middle, high, low, middle], axis=axis)
    second = jnp.concatenate([high2, middle2, high2, low2, high2, middle2], axis=axis)
    return first.astype(BF16), second.astype(BF16)


def fold(products, rank):
    return products[:rank] + (products[rank : 2 * rank] + products[2 * rank : 3 * rank])


def left_kernel(gradient, error, start, out, gradient_here, error_here, start_here, arrived):
    first = pltpu.make_async_copy(start, start_here, arrived.at[0])
    first.start()
    columns = gradient.shape[1]
    edges = [0, columns // 4, columns * 5 // 8, columns]
    spans = list(zip(edges[:-1], edges[1:]))
    copies = []
    for index, (low, high) in enumerate(spans):
        pair = []
        for which, (source, target) in enumerate(((gradient, gradient_here), (error, error_here))):
            span = pl.ds(low, high - low)
            copy = pltpu.make_async_copy(source.at[:, span], target.at[:, span], arrived.at[1 + 2 * index + which])
            copy.start()
            pair.append(copy)
        copies.append(pair)
    first.wait()
    cut = pieces(start_here[...]).astype(F32).T.astype(BF16)
    total = 0.0
    for (low, high), pair in zip(spans, copies):
        for copy in pair:
            copy.wait()
        total += jnp.dot(gradient_here[:, low:high], cut[low:high], preferred_element_type=F32) + jnp.dot(
            error_here[:, low:high], cut[low:high], preferred_element_type=F32
        )
    left = fold(total.T, start.shape[0])
    for copy in range(out.shape[0]):
        out[copy] = left


def left_terms(gradient, error, start, replicas):
    rows, columns = gradient.shape
    rank = start.shape[0]
    return pl.pallas_call(
        left_kernel,
        out_shape=(
            pltpu.VMEM((replicas, rank, rows), F32),
            pltpu.VMEM((rows, columns), BF16),
            pltpu.VMEM((rows, columns), BF16),
        ),
        in_specs=[pl.BlockSpec(memory_space=pltpu.HBM)] * 3,
        out_specs=(VMEM, VMEM, VMEM),
        scratch_shapes=[pltpu.VMEM((rank, columns), F32), pltpu.SemaphoreType.DMA((7,))],
        compiler_params=SMALL,
        name="left_terms",
    )(*(pltpu.with_memory_space_constraint(array, pltpu.HBM) for array in (gradient, error, start)))


def raw_kernel(parts, gradient, error, sent, left_out):
    left = jnp.sum(parts[...], axis=0)
    left_out[...] = left
    rank, rows = left.shape
    none = jnp.zeros((GAP - rank, rows), F32)
    filled = jnp.concatenate([left, none] * (LANES // GAP), axis=0)
    gram = lax.dot_general(left, filled, (((1,), (1,)), ((), ())), precision=HIGH, preferred_element_type=F32)
    gram_row = jnp.sum(jnp.where(own_lanes(gram.shape), gram, 0.0), axis=0, keepdims=True)
    cut = pieces(left)
    step = 2 * LANES
    high = rank + 1
    for pair in range(gradient.shape[1] // step):
        span = slice(pair * step, (pair + 1) * step)
        total = jnp.dot(cut, gradient[:, span], preferred_element_type=F32)
        total += jnp.dot(cut, error[:, span], preferred_element_type=F32)
        total = fold(total, rank)
        for half in range(2):
            place = ORDERS["near"].index(ORDERS["back"][2 * pair + half])
            start = place * high
            sent[start : start + rank, :] = total[:, half * LANES : (half + 1) * LANES]
            sent[start + rank : start + high, :] = gram_row


def own_lanes(shape):
    row = lax.broadcasted_iota(jnp.int32, shape, 0)
    lane = lax.broadcasted_iota(jnp.int32, shape, 1)
    return (lane >= row * GAP) & (lane < (row + 1) * GAP)


def raw_terms(parts, gradient, error, blocks):
    _, rank, rows = parts.shape
    return pl.pallas_call(
        raw_kernel,
        out_shape=(
            pltpu.VMEM((blocks * (rank + 1), LANES), F32),
            pltpu.VMEM((rank, rows), F32),
        ),
        in_specs=[VMEM, VMEM, VMEM],
        out_specs=(VMEM, VMEM),
        compiler_params=SMALL,
        name="raw_terms",
    )(parts, gradient, error)


def sum_blocks(parts, count):
    high = parts.shape[0] // count
    terms = [parts[index * high : (index + 1) * high, :] for index in range(count)]
    while len(terms) > 1:
        terms = [one + other for one, other in zip(terms[::2], terms[1::2])]
    return terms[0]


def sum_kernel(count, parts, out):
    total = sum_blocks(parts, count)
    high = total.shape[0]
    for copy in range(out.shape[0] // high):
        out[copy * high : (copy + 1) * high, :] = total


def sum_copies(parts, count, copies):
    high = parts.shape[0] // count
    return pl.pallas_call(
        functools.partial(sum_kernel, count),
        out_shape=pltpu.VMEM((copies * high, LANES), F32),
        in_specs=[VMEM],
        out_specs=VMEM,
        compiler_params=SMALL,
        name="sum_copies",
    )(parts)


def solve_kernel(replicas, count, parts, left, out, left_out):
    total = sum_blocks(parts, count) * (1.0 / replicas)
    rank, rows = left.shape
    gram = jnp.broadcast_to(total[rank:], (rank, LANES))
    gram = jnp.where(own_lanes(gram.shape), gram, 0.0)
    shift = LANES // 2
    while shift >= GAP:
        gram = gram + pltpu.roll(gram, shift, 1)
        shift //= 2
    spread = [jnp.broadcast_to(gram[:, column : column + 1], (rank, LANES)) for column in range(rank)]
    values = [left[:, low : low + LANES] for low in range(0, rows, LANES)] + [total[:rank]]
    index = lax.broadcasted_iota(jnp.int32, (rank, LANES), 0)
    for step in range(rank):
        scale = lax.rsqrt(spread[step][step : step + 1, :])
        factor = spread[step] * scale

        def eliminate(table):
            pivot = table[step : step + 1, :] * scale
            return jnp.where(index > step, table - factor * pivot, jnp.where(index == step, pivot, table))

        spread = spread[: step + 1] + [eliminate(table) for table in spread[step + 1 :]]
        values = [eliminate(table) for table in values]
    for place, low in enumerate(range(0, rows, LANES)):
        left_out[:, low : low + LANES] = values[place]
    for copy in range(out.shape[0]):
        out[copy] = values[-1]


def solve(parts, count, left, blocks, replicas):
    rank = left.shape[0]
    return pl.pallas_call(
        functools.partial(solve_kernel, replicas, count),
        out_shape=(
            pltpu.VMEM((blocks, rank, LANES), F32),
            pltpu.VMEM(left.shape, F32),
        ),
        in_specs=[VMEM, VMEM],
        out_specs=(VMEM, VMEM),
        compiler_params=SMALL,
        name="solve",
    )(parts, left)


def update_kernel(parts, left, update, left_out, right):
    blocks, _, width = parts.shape
    here = 0
    for axis in DP:
        here = here * lax.axis_size(axis) + lax.axis_index(axis)
    first, second = stacked(left[...], parts[here], 0)
    update[...] = lax.dot_general(first, second, (((0,), (0,)), ((), ())), preferred_element_type=F32)
    left_out[...] = left[...]
    for block in range(blocks):
        right[:, block * width : (block + 1) * width] = parts[block]


def finish(parts, left):
    blocks, rank, width = parts.shape
    return pl.pallas_call(
        update_kernel,
        out_shape=(
            jax.ShapeDtypeStruct((left.shape[1], width), F32),
            jax.ShapeDtypeStruct(left.shape, F32),
            jax.ShapeDtypeStruct((rank, blocks * width), F32),
        ),
        in_specs=[VMEM, VMEM],
        out_specs=(VMEM, VMEM, VMEM),
        compiler_params=SMALL,
        name="update",
    )(parts, left)


def exchange(blocks, axes, order):
    if order == "far":
        return lax.all_to_all(blocks, ALL, 0, 0, axis_index_groups=ORDERS[order])
    return lax.all_to_all(blocks, axes, 0, 0, axis_index_groups=[ORDERS[order]])


def exchange_rows(rows, axes, order):
    count = math.prod(lax.axis_size(axis) for axis in axes)
    high = rows.shape[0] // count
    return exchange(rows.reshape(count, high, 1, LANES), axes, order).reshape(rows.shape)


def on_device(gradient, error_buffer, right_start):
    replicas, blocks, far = (math.prod(lax.axis_size(axis) for axis in axes) for axes in (DP, NEAR, FAR))
    lefts, gradient, error = left_terms(gradient[0], error_buffer[0], right_start, replicas)
    raws, left_sum = raw_terms(exchange(lefts, DP, "left"), gradient, error, blocks)
    sums = sum_copies(exchange_rows(raws, NEAR, "near"), blocks, far)
    rights, left_factor = solve(exchange_rows(sums, FAR, "far"), far, left_sum, blocks, replicas)
    return finish(exchange(rights, NEAR, "back"), left_factor)


def solution(mesh):
    split = Mesh(mesh.devices.reshape(4, 2, 4, 4, 2, 2), ("yh", "yl", "x", "zh", "zl", "core"))
    return jax.shard_map(
        on_device,
        mesh=split,
        in_specs=(P(DP, TENSOR, None), P(DP, TENSOR, None), P()),
        out_specs=(P(TENSOR, DP), P(None, TENSOR), P()),
        check_vma=False,
    )
```
